32 devices in a mesh: row: 4 (over y, x), blk: 8 (over z, core).
Axes of the slice: x: 2, y: 2, z: 4, core: 2. Of those that a mesh axis runs over, the one named last changes fastest.
Arguments:
- inputs: bfloat16 [4, 2048, 2048], P('row', 'blk'), may hold values from -6 to 6
- cotangent: bfloat16 [4, 2048, 2048], P('row', 'blk'), may hold values from -6 to 6
- doc_lengths: int32 [4, 8], P('row'), may hold values from 1 to 2041, as said below
- norm_gains: float32 [2, 2048], P(None, ('row', 'blk')), may hold values from 0.5 to 1.5
- gain_first: float32 [2, 2048], P(None, ('row', 'blk')), may hold values from -56 to 56
- gain_second: float32 [2, 2048], P(None, ('row', 'blk')), may hold values from 1228.8 to 4915.2
- query_weight: float32 [32, 512, 256], P(('row', 'blk')), may hold values from -0.125 to 0.125
- query_left: float32 [32, 512, 512], P(('row', 'blk')), as said below
- query_right: float32 [32, 256, 256], P(('row', 'blk')), as said below
- query_leftroot: float32 [32, 512, 512], P(('row', 'blk')), as said below
- query_rightroot: float32 [32, 256, 256], P(('row', 'blk')), as said below
- key_weight: float32 [32, 256, 128], P(('row', 'blk')), may hold values from -0.125 to 0.125
- key_left: float32 [32, 256, 256], P(('row', 'blk')), as said below
- key_right: float32 [32, 128, 128], P(('row', 'blk')), as said below
- key_leftroot: float32 [32, 256, 256], P(('row', 'blk')), as said below
- key_rightroot: float32 [32, 128, 128], P(('row', 'blk')), as said below
- value_weight: float32 [32, 256, 128], P(('row', 'blk')), may hold values from -0.125 to 0.125
- value_left: float32 [32, 256, 256], P(('row', 'blk')), as said below
- value_right: float32 [32, 128, 128], P(('row', 'blk')), as said below
- value_leftroot: float32 [32, 256, 256], P(('row', 'blk')), as said below
- value_rightroot: float32 [32, 128, 128], P(('row', 'blk')), as said below
- output_weight: float32 [32, 256, 512], P(('row', 'blk')), may hold values from -4 to 4
- output_left: float32 [32, 256, 256], P(('row', 'blk')), as said below
- output_right: float32 [32, 512, 512], P(('row', 'blk')), as said below
- output_leftroot: float32 [32, 256, 256], P(('row', 'blk')), as said below
- output_rightroot: float32 [32, 512, 512], P(('row', 'blk')), as said below
- gate_weight: float32 [32, 512, 1024], P(('row', 'blk')), may hold values from -0.125 to 0.125
- gate_left: float32 [32, 512, 512], P(('row', 'blk')), as said below
- gate_right: float32 [32, 1024, 1024], P(('row', 'blk')), as said below
- gate_leftroot: float32 [32, 512, 512], P(('row', 'blk')), as said below
- gate_rightroot: float32 [32, 1024, 1024], P(('row', 'blk')), as said below
- up_weight: float32 [32, 512, 1024], P(('row', 'blk')), may hold values from -0.125 to 0.125
- up_left: float32 [32, 512, 512], P(('row', 'blk')), as said below
- up_right: float32 [32, 1024, 1024], P(('row', 'blk')), as said below
- up_leftroot: float32 [32, 512, 512], P(('row', 'blk')), as said below
- up_rightroot: float32 [32, 1024, 1024], P(('row', 'blk')), as said below
- down_weight: float32 [32, 1024, 512], P(('row', 'blk')), may hold values from -0.0625 to 0.0625
- down_left: float32 [32, 1024, 1024], P(('row', 'blk')), as said below
- down_right: float32 [32, 512, 512], P(('row', 'blk')), as said below
- down_leftroot: float32 [32, 1024, 1024], P(('row', 'blk')), as said below
- down_rightroot: float32 [32, 512, 512], P(('row', 'blk')), as said below
Outputs:
- block_out: bfloat16 [4, 2048, 2048], P('row', 'blk')
- input_grad: float32 [4, 2048, 2048], P('row', 'blk')
- query_grad: float32 [32, 512, 256], P(('row', 'blk'))
- query_new: float32 [32, 512, 256], P(('row', 'blk'))
- query_leftnew: float32 [32, 512, 512], P(('row', 'blk'))
- query_rightnew: float32 [32, 256, 256], P(('row', 'blk'))
- key_grad: float32 [32, 256, 128], P(('row', 'blk'))
- key_new: float32 [32, 256, 128], P(('row', 'blk'))
- key_leftnew: float32 [32, 256, 256], P(('row', 'blk'))
- key_rightnew: float32 [32, 128, 128], P(('row', 'blk'))
- value_grad: float32 [32, 256, 128], P(('row', 'blk'))
- value_new: float32 [32, 256, 128], P(('row', 'blk'))
- value_leftnew: float32 [32, 256, 256], P(('row', 'blk'))
- value_rightnew: float32 [32, 128, 128], P(('row', 'blk'))
- output_grad: float32 [32, 256, 512], P(('row', 'blk'))
- output_new: float32 [32, 256, 512], P(('row', 'blk'))
- output_leftnew: float32 [32, 256, 256], P(('row', 'blk'))
- output_rightnew: float32 [32, 512, 512], P(('row', 'blk'))
- gate_grad: float32 [32, 512, 1024], P(('row', 'blk'))
- gate_new: float32 [32, 512, 1024], P(('row', 'blk'))
- gate_leftnew: float32 [32, 512, 512], P(('row', 'blk'))
- gate_rightnew: float32 [32, 1024, 1024], P(('row', 'blk'))
- up_grad: float32 [32, 512, 1024], P(('row', 'blk'))
- up_new: float32 [32, 512, 1024], P(('row', 'blk'))
- up_leftnew: float32 [32, 512, 512], P(('row', 'blk'))
- up_rightnew: float32 [32, 1024, 1024], P(('row', 'blk'))
- down_grad: float32 [32, 1024, 512], P(('row', 'blk'))
- down_new: float32 [32, 1024, 512], P(('row', 'blk'))
- down_leftnew: float32 [32, 1024, 1024], P(('row', 'blk'))
- down_rightnew: float32 [32, 512, 512], P(('row', 'blk'))
- gain_moment: float32 [2, 2048], P(None, ('row', 'blk'))
- gain_square: float32 [2, 2048], P(None, ('row', 'blk'))
- gains_new: float32 [2, 2048], P(None, ('row', 'blk'))
The draws below stay inside these ranges and needn't reach their ends.
Inputs may be any that keep to these rules, and one draw needn't show every extreme that they name: `doc_lengths`: the 8 lengths of each row sum to 2048. `query_left`: symmetric, one matrix for each block. `query_right`: symmetric, one matrix for each block. `query_leftroot`: symmetric, one matrix for each block. `query_rightroot`: symmetric, one matrix for each block. `key_left`: symmetric, one matrix for each block. `key_right`: symmetric, one matrix for each block. `key_leftroot`: symmetric, one matrix for each block. `key_rightroot`: symmetric, one matrix for each block. `value_left`: symmetric, one matrix for each block. `value_right`: symmetric, one matrix for each block. `value_leftroot`: symmetric, one matrix for each block. `value_rightroot`: symmetric, one matrix for each block. `output_left`: symmetric, one matrix for each block. `output_right`: symmetric, one matrix for each block. `output_leftroot`: symmetric, one matrix for each block. `output_rightroot`: symmetric, one matrix for each block. `gate_left`: symmetric, one matrix for each block. `gate_right`: symmetric, one matrix for each block. `gate_leftroot`: symmetric, one matrix for each block. `gate_rightroot`: symmetric, one matrix for each block. `up_left`: symmetric, one matrix for each block. `up_right`: symmetric, one matrix for each block. `up_leftroot`: symmetric, one matrix for each block. `up_rightroot`: symmetric, one matrix for each block. `down_left`: symmetric, one matrix for each block. `down_right`: symmetric, one matrix for each block. `down_leftroot`: symmetric, one matrix for each block. `down_rightroot`: symmetric, one matrix for each block.
All inputs are finite; a program needn't handle non-finite values.
Results may differ from the reference program's by a relative error of at most 0.023.
Values may be sent and summed in bfloat16 or wider, within the bound.
No kernel may reach another device: no remote copies, remote signals or barrier semaphores. Data moves between devices by JAX's collectives and lax.ppermute only.
A program may use at most 640 MiB of HBM per device.

```python
import math
import jax
import jax.numpy as jnp
from jax import lax

D = 2048
HEADS = 32
KV_HEADS = 8
HEAD_DIM = 64
FF = 8192
TOK_DEV = 256
NDOCS = 8
STEP = 10
ROWS = 4
SEQ = 2048
TOKENS = 8192
Q_ROWS = 512
Q_COLS = 256
KV_ROWS = 256
KV_COLS = 128
O_ROWS = 256
O_COLS = 512
F_ROWS = 512
F_COLS = 1024
DN_ROWS = 1024
DN_COLS = 512
N_ROW = 4
N_BLK = 8
DEVICES = 32


STAT_RATIO = 0.05 / 0.95


STEP_RATE = 0.5


VALUE_BOOST = 6.0


OUTPUT_BOOST = 4.0


def stat_draw(key, size, scale):
    spread = jnp.exp(jax.random.uniform(key, (DEVICES, size), jnp.float32, 0.0, math.log(4.0)))
    return jnp.eye(size, dtype=jnp.float32)[None, :, :] * (scale * spread)[:, None, :]


def root_draw(key, size, scale):
    first_key, second_key = jax.random.split(key)
    diagonal = jax.random.uniform(first_key, (DEVICES, size), jnp.float32, 1.0, 2.0)
    noise_part = jax.random.normal(second_key, (DEVICES, size, size), jnp.float32)
    symmetric = 0.2 / math.sqrt(size) * (noise_part + jnp.swapaxes(noise_part, 1, 2))
    return scale * (jnp.eye(size, dtype=jnp.float32)[None, :, :] * diagonal[:, None, :] + symmetric)


def root_scale(spread_weight, grad_square):
    return math.sqrt(spread_weight / (STEP_RATE * math.sqrt(grad_square))) / 1.5


def draw_doc_lengths(key, part):
    key = jax.random.fold_in(key, 1)
    first_key, second_key, third_key = jax.random.split(key, 3)
    others = jax.random.randint(first_key, (ROWS, NDOCS), 1, TOK_DEV // NDOCS + 1, dtype=jnp.int32)
    special = jax.random.randint(third_key, (), 0, ROWS, dtype=jnp.int32)
    row_ids = jnp.arange(ROWS, dtype=jnp.int32)[:, None]
    others = jnp.where(row_ids == special, 1, others).astype(jnp.int32)
    chosen = jax.random.randint(second_key, (ROWS, 1), 0, NDOCS, dtype=jnp.int32)
    slot_ids = jnp.arange(NDOCS, dtype=jnp.int32)[None, :]
    others_sum = jnp.sum(jnp.where(slot_ids == chosen, 0, others), axis=-1, keepdims=True)
    return jnp.where(slot_ids == chosen, SEQ - others_sum, others).astype(jnp.int32)


def draw_query_left(key, part):
    key = jax.random.fold_in(key, 11)
    return stat_draw(key, Q_ROWS, STAT_RATIO * Q_COLS * TOKENS)


def draw_query_right(key, part):
    key = jax.random.fold_in(key, 12)
    return stat_draw(key, Q_COLS, STAT_RATIO * Q_ROWS * TOKENS)


def draw_query_leftroot(key, part):
    key = jax.random.fold_in(key, 13)
    return root_draw(key, Q_ROWS, root_scale(D ** (-0.5), TOKENS))


def draw_query_rightroot(key, part):
    key = jax.random.fold_in(key, 14)
    return root_draw(key, Q_COLS, root_scale(D ** (-0.5), TOKENS))


def draw_key_left(key, part):
    key = jax.random.fold_in(key, 21)
    return stat_draw(key, KV_ROWS, STAT_RATIO * KV_COLS * TOKENS)


def draw_key_right(key, part):
    key = jax.random.fold_in(key, 22)
    return stat_draw(key, KV_COLS, STAT_RATIO * KV_ROWS * TOKENS)


def draw_key_leftroot(key, part):
    key = jax.random.fold_in(key, 23)
    return root_draw(key, KV_ROWS, root_scale(D ** (-0.5), TOKENS))


def draw_key_rightroot(key, part):
    key = jax.random.fold_in(key, 24)
    return root_draw(key, KV_COLS, root_scale(D ** (-0.5), TOKENS))


def draw_value_left(key, part):
    key = jax.random.fold_in(key, 31)
    return stat_draw(key, KV_ROWS, VALUE_BOOST * STAT_RATIO * KV_COLS * TOKENS)


def draw_value_right(key, part):
    key = jax.random.fold_in(key, 32)
    return stat_draw(key, KV_COLS, VALUE_BOOST * STAT_RATIO * KV_ROWS * TOKENS)


def draw_value_leftroot(key, part):
    key = jax.random.fold_in(key, 33)
    return root_draw(key, KV_ROWS, root_scale(D ** (-0.5), TOKENS))


def draw_value_rightroot(key, part):
    key = jax.random.fold_in(key, 34)
    return root_draw(key, KV_COLS, root_scale(D ** (-0.5), TOKENS))


def draw_output_left(key, part):
    key = jax.random.fold_in(key, 41)
    return stat_draw(key, O_ROWS, STAT_RATIO * O_COLS * 2.0 * TOKENS / SEQ)


def draw_output_right(key, part):
    key = jax.random.fold_in(key, 42)
    return stat_draw(key, O_COLS, OUTPUT_BOOST * STAT_RATIO * O_ROWS * 2.0 * TOKENS / SEQ)


def draw_output_leftroot(key, part):
    key = jax.random.fold_in(key, 43)
    return root_draw(key, O_ROWS, root_scale(max(1, 2 * D // SEQ) ** (-0.5), 2.0 * TOKENS / SEQ))


def draw_output_rightroot(key, part):
    key = jax.random.fold_in(key, 44)
    return root_draw(key, O_COLS, root_scale(max(1, 2 * D // SEQ) ** (-0.5), 2.0 * TOKENS / SEQ))


def draw_gate_left(key, part):
    key = jax.random.fold_in(key, 51)
    return stat_draw(key, F_ROWS, STAT_RATIO * F_COLS * 0.1 * TOKENS)


def draw_gate_right(key, part):
    key = jax.random.fold_in(key, 52)
    return stat_draw(key, F_COLS, STAT_RATIO * F_ROWS * 0.1 * TOKENS)


def draw_gate_leftroot(key, part):
    key = jax.random.fold_in(key, 53)
    return root_draw(key, F_ROWS, root_scale(D ** (-0.5), 0.1 * TOKENS))


def draw_gate_rightroot(key, part):
    key = jax.random.fold_in(key, 54)
    return root_draw(key, F_COLS, root_scale(D ** (-0.5), 0.1 * TOKENS))


def draw_up_left(key, part):
    key = jax.random.fold_in(key, 61)
    return stat_draw(key, F_ROWS, STAT_RATIO * F_COLS * 0.1 * TOKENS)


def draw_up_right(key, part):
    key = jax.random.fold_in(key, 62)
    return stat_draw(key, F_COLS, STAT_RATIO * F_ROWS * 0.1 * TOKENS)


def draw_up_leftroot(key, part):
    key = jax.random.fold_in(key, 63)
    return root_draw(key, F_ROWS, root_scale(D ** (-0.5), 0.1 * TOKENS))


def draw_up_rightroot(key, part):
    key = jax.random.fold_in(key, 64)
    return root_draw(key, F_COLS, root_scale(D ** (-0.5), 0.1 * TOKENS))


def draw_down_left(key, part):
    key = jax.random.fold_in(key, 71)
    return stat_draw(key, DN_ROWS, STAT_RATIO * DN_COLS * 0.36 * TOKENS)


def draw_down_right(key, part):
    key = jax.random.fold_in(key, 72)
    return stat_draw(key, DN_COLS, STAT_RATIO * DN_ROWS * 0.36 * TOKENS)


def draw_down_leftroot(key, part):
    key = jax.random.fold_in(key, 73)
    return root_draw(key, DN_ROWS, root_scale(FF ** (-0.5), 0.36 * TOKENS))


def draw_down_rightroot(key, part):
    key = jax.random.fold_in(key, 74)
    return root_draw(key, DN_COLS, root_scale(FF ** (-0.5), 0.36 * TOKENS))


def level_of(own_key, extent, shards, least, high):
    loudness, own = 1.0, jax.random.fold_in(own_key, 6)
    for dim, parts in shards:
        steps = jnp.exp(jax.random.uniform(jax.random.fold_in(own, dim), (parts,), jnp.float32, least / len(shards), high / len(shards)))
        loudness = loudness * jnp.repeat(steps, extent[dim] // parts).reshape([-1 if axis == dim else 1 for axis in range(len(extent))])
    return loudness


def centred(key, dims, deviation, bound, cuts=(), held_as=jnp.bfloat16):
    entries = jax.random.normal(key, dims, jnp.float32) * deviation
    if len(cuts) > 0:
        entries = level_of(key, dims, cuts, -0.22, 0.18) * entries
    return jnp.clip(entries, min=-bound, max=bound).astype(held_as)


def setup_inputs(seed: int = 0) -> dict:
    key_of = jax.random.split(jax.random.key(seed), 42)
    return {
        "inputs": centred(key_of[0], (ROWS, SEQ, D), 1.0, 6.0, ((0, 4), (1, 8))),
        "cotangent": centred(key_of[1], (ROWS, SEQ, D), 1.0, 6.0, ((0, 4), (1, 8))),
        "doc_lengths": draw_doc_lengths(jax.random.fold_in(key_of[41], 71), 0),
        "norm_gains": jnp.clip(1.0 + 0.1 * jax.random.normal(key_of[3], (2, D), jnp.float32), 0.5, 1.5),
        "gain_first": centred(key_of[4], (2, D), (0.1 * TOKENS ** 0.5), 56.0, ((1, 32),), jnp.float32),
        "gain_second": jnp.clip(jnp.exp(math.log(4915.2) - 1.3862944 * jax.random.uniform(key_of[5], (2, D), jnp.float32) ** level_of(key_of[5], (2, D), ((1, 32),), -0.2, 0.2)), 1228.8, 4915.2),
        "query_weight": centred(key_of[6], (DEVICES, Q_ROWS, Q_COLS), D ** -0.5, 0.125, ((0, 32),), jnp.float32),
        "query_left": draw_query_left(jax.random.fold_in(key_of[41], 71), 0),
        "query_right": draw_query_right(jax.random.fold_in(key_of[41], 71), 0),
        "query_leftroot": draw_query_leftroot(jax.random.fold_in(key_of[41], 71), 0),
        "query_rightroot": draw_query_rightroot(jax.random.fold_in(key_of[41], 71), 0),
        "key_weight": centred(key_of[11], (DEVICES, KV_ROWS, KV_COLS), D ** -0.5, 0.125, ((0, 32),), jnp.float32),
        "key_left": draw_key_left(jax.random.fold_in(key_of[41], 71), 0),
        "key_right": draw_key_right(jax.random.fold_in(key_of[41], 71), 0),
        "key_leftroot": draw_key_leftroot(jax.random.fold_in(key_of[41], 71), 0),
        "key_rightroot": draw_key_rightroot(jax.random.fold_in(key_of[41], 71), 0),
        "value_weight": centred(key_of[16], (DEVICES, KV_ROWS, KV_COLS), D ** -0.5, 0.125, ((0, 32),), jnp.float32),
        "value_left": draw_value_left(jax.random.fold_in(key_of[41], 71), 0),
        "value_right": draw_value_right(jax.random.fold_in(key_of[41], 71), 0),
        "value_leftroot": draw_value_leftroot(jax.random.fold_in(key_of[41], 71), 0),
        "value_rightroot": draw_value_rightroot(jax.random.fold_in(key_of[41], 71), 0),
        "output_weight": centred(key_of[21], (DEVICES, O_ROWS, O_COLS), (max(1, 2 * D // SEQ)) ** -0.5, 4.0, ((0, 32),), jnp.float32),
        "output_left": draw_output_left(jax.random.fold_in(key_of[41], 71), 0),
        "output_right": draw_output_right(jax.random.fold_in(key_of[41], 71), 0),
        "output_leftroot": draw_output_leftroot(jax.random.fold_in(key_of[41], 71), 0),
        "output_rightroot": draw_output_rightroot(jax.random.fold_in(key_of[41], 71), 0),
        "gate_weight": centred(key_of[26], (DEVICES, F_ROWS, F_COLS), D ** -0.5, 0.125, ((0, 32),), jnp.float32),
        "gate_left": draw_gate_left(jax.random.fold_in(key_of[41], 71), 0),
        "gate_right": draw_gate_right(jax.random.fold_in(key_of[41], 71), 0),
        "gate_leftroot": draw_gate_leftroot(jax.random.fold_in(key_of[41], 71), 0),
        "gate_rightroot": draw_gate_rightroot(jax.random.fold_in(key_of[41], 71), 0),
        "up_weight": centred(key_of[31], (DEVICES, F_ROWS, F_COLS), D ** -0.5, 0.125, ((0, 32),), jnp.float32),
        "up_left": draw_up_left(jax.random.fold_in(key_of[41], 71), 0),
        "up_right": draw_up_right(jax.random.fold_in(key_of[41], 71), 0),
        "up_leftroot": draw_up_leftroot(jax.random.fold_in(key_of[41], 71), 0),
        "up_rightroot": draw_up_rightroot(jax.random.fold_in(key_of[41], 71), 0),
        "down_weight": centred(key_of[36], (DEVICES, DN_ROWS, DN_COLS), FF ** -0.5, 0.0625, ((0, 32),), jnp.float32),
        "down_left": draw_down_left(jax.random.fold_in(key_of[41], 71), 0),
        "down_right": draw_down_right(jax.random.fold_in(key_of[41], 71), 0),
        "down_leftroot": draw_down_leftroot(jax.random.fold_in(key_of[41], 71), 0),
        "down_rightroot": draw_down_rightroot(jax.random.fold_in(key_of[41], 71), 0),
    }


NORM_EPSILON = 1e-05
ROPE_THETA = 500000.0
ROPE_FACTOR = 32.0
LOW_FACTOR = 1.0
HIGH_FACTOR = 4.0
BASE_SPAN = 8192.0
SCORE_SCALE = 0.125
MASKED = -1e+30
SHAMPOO_DECAY = 0.95
SHAMPOO_RATE = 0.5
ADAM_RATE = 1.0
ADAM_FIRST = 0.9
ADAM_SECOND = 0.95
ADAM_EPSILON = 1e-08
HIGHEST = lax.Precision.HIGHEST

@jax.custom_vjp
def low(v):
    return lax.optimization_barrier(v.astype(jnp.bfloat16)).astype(jnp.float32)

@jax.custom_vjp
def low_back(v):
    return v

def low_keep(v):
    return (low(v), None)

def low_pass(kept, grad):
    return (grad,)

def back_keep(v):
    return (v, None)

def back_low(kept, grad):
    return (low(grad),)
low.defvjp(low_keep, low_pass)
low_back.defvjp(back_keep, back_low)

def rope_rates():
    exponents = jnp.arange(0, HEAD_DIM, 2).astype(jnp.float32) / HEAD_DIM
    base_rates = 1.0 / ROPE_THETA ** exponents
    wavelength = 2.0 * math.pi / base_rates
    smooth = (BASE_SPAN / wavelength - LOW_FACTOR) / (HIGH_FACTOR - LOW_FACTOR)
    blended = (1.0 - smooth) * base_rates / ROPE_FACTOR + smooth * base_rates
    longer = jnp.where(wavelength > BASE_SPAN / LOW_FACTOR, base_rates / ROPE_FACTOR, blended)
    return jnp.where(wavelength < BASE_SPAN / HIGH_FACTOR, base_rates, longer)

def rotate(vectors, cos_table, sin_table):
    half_dim = vectors.shape[-1] // 2
    former = vectors[..., :half_dim]
    latter = vectors[..., half_dim:]
    return jnp.concatenate([former * cos_table - latter * sin_table, latter * cos_table + former * sin_table], axis=-1)

def to_full(blocks, rows_first):
    size_in = blocks.shape[1]
    size_out = blocks.shape[2]
    shaped = blocks.reshape(N_ROW, N_BLK, size_in, size_out)
    if rows_first:
        return shaped.transpose(0, 2, 1, 3).reshape(N_ROW * size_in, N_BLK * size_out)
    return shaped.transpose(1, 2, 0, 3).reshape(N_BLK * size_in, N_ROW * size_out)

def to_blocks(full, rows_first, size_in, size_out):
    if rows_first:
        return full.reshape(N_ROW, size_in, N_BLK, size_out).transpose(0, 2, 1, 3).reshape(N_ROW * N_BLK, size_in, size_out)
    return full.reshape(N_BLK, size_in, N_ROW, size_out).transpose(2, 0, 1, 3).reshape(N_ROW * N_BLK, size_in, size_out)

def shampoo_step(gradient, master, left, right, left_root, right_root):
    left_new = SHAMPOO_DECAY * left + (1.0 - SHAMPOO_DECAY) * jnp.einsum('nab,ncb->nac', gradient, gradient, precision=HIGHEST)
    right_new = SHAMPOO_DECAY * right + (1.0 - SHAMPOO_DECAY) * jnp.einsum('nab,nac->nbc', gradient, gradient, precision=HIGHEST)
    turned = jnp.einsum('nab,nbc->nac', left_root, gradient, precision=HIGHEST)
    direction = jnp.einsum('nab,nbc->nac', turned, right_root, precision=HIGHEST)
    return (gradient, master - SHAMPOO_RATE * direction, left_new, right_new)

def adam_step(gradient, gains, first, second):
    first_new = ADAM_FIRST * first + (1.0 - ADAM_FIRST) * gradient
    second_new = ADAM_SECOND * second + (1.0 - ADAM_SECOND) * gradient * gradient
    corrected_first = first_new / (1.0 - ADAM_FIRST ** STEP)
    corrected_second = second_new / (1.0 - ADAM_SECOND ** STEP)
    return (first_new, second_new, gains - ADAM_RATE * corrected_first / (jnp.sqrt(corrected_second) + ADAM_EPSILON))

def attend_row(queries, key_rows, value_rows, begins):
    block_rows = math.gcd(SEQ, 512)
    key_index = jnp.arange(SEQ, dtype=jnp.int32)

    def attend_block(number):
        offset = number * block_rows
        part = lax.dynamic_slice_in_dim(queries, offset, block_rows, 0)
        begin_part = lax.dynamic_slice_in_dim(begins, offset, block_rows, 0)
        query_index = offset + jnp.arange(block_rows, dtype=jnp.int32)
        scores = SCORE_SCALE * jnp.einsum('tkgd,skd->kgts', part, key_rows, precision=HIGHEST)
        scores = low_back(scores)
        allowed = (key_index[None, :] >= begin_part[:, None]) & (key_index[None, :] <= query_index[:, None])
        probabilities = jax.nn.softmax(jnp.where(allowed, scores, MASKED), axis=-1)
        return jnp.einsum('kgts,skd->tkgd', low(probabilities), value_rows, precision=HIGHEST)
    pieces = lax.map(jax.checkpoint(attend_block), jnp.arange(SEQ // block_rows, dtype=jnp.int32))
    return pieces.reshape(SEQ, HEADS * HEAD_DIM)

def reference(inputs, cotangent, doc_lengths, norm_gains, gain_first, gain_second, query_weight, query_left, query_right, query_leftroot, query_rightroot, key_weight, key_left, key_right, key_leftroot, key_rightroot, value_weight, value_left, value_right, value_leftroot, value_rightroot, output_weight, output_left, output_right, output_leftroot, output_rightroot, gate_weight, gate_left, gate_right, gate_leftroot, gate_rightroot, up_weight, up_left, up_right, up_leftroot, up_rightroot, down_weight, down_left, down_right, down_leftroot, down_rightroot):
    token_count = ROWS * SEQ
    group_size = HEADS // KV_HEADS
    positions_row = jnp.arange(SEQ, dtype=jnp.int32)
    doc_ends = jnp.cumsum(doc_lengths, axis=-1).astype(jnp.int32)
    doc_starts = (doc_ends - doc_lengths).astype(jnp.int32)
    inside = (positions_row[None, :, None] >= doc_starts[:, None, :]) & (positions_row[None, :, None] < doc_ends[:, None, :])
    begins = lax.optimization_barrier(jnp.sum(jnp.where(inside, doc_starts[:, None, :], 0), axis=-1)).astype(jnp.int32)
    offsets = (positions_row[None, :] - begins).reshape(token_count).astype(jnp.float32)
    angles = offsets[:, None] * rope_rates()[None, :]
    cos_table = jnp.cos(angles)[:, None, :]
    sin_table = jnp.sin(angles)[:, None, :]

    def forward_layer(resid, query_full, key_full, value_full, output_full, gate_full, up_full, down_full, gains):
        gains_low = low(gains)
        normed_first = resid * lax.rsqrt(lax.optimization_barrier(jnp.mean(resid * resid, axis=-1, keepdims=True)) + NORM_EPSILON)
        scaled_first = low(normed_first * gains_low[0])
        query_pre = low_back(jnp.dot(scaled_first, low(query_full), precision=HIGHEST, preferred_element_type=jnp.float32))
        key_pre = low_back(jnp.dot(scaled_first, low(key_full), precision=HIGHEST, preferred_element_type=jnp.float32))
        value_rows = low_back(low(jnp.dot(scaled_first, low(value_full), precision=HIGHEST, preferred_element_type=jnp.float32)))
        queries = low(rotate(query_pre.reshape(token_count, HEADS, HEAD_DIM), cos_table, sin_table))
        key_rows = low(rotate(key_pre.reshape(token_count, KV_HEADS, HEAD_DIM), cos_table, sin_table))
        attended = lax.map(lambda row_items: attend_row(row_items[0], row_items[1], row_items[2], row_items[3]), (queries.reshape(ROWS, SEQ, KV_HEADS, group_size, HEAD_DIM), key_rows.reshape(ROWS, SEQ, KV_HEADS, HEAD_DIM), value_rows.reshape(ROWS, SEQ, KV_HEADS, HEAD_DIM), begins))
        attended = low_back(low(attended.reshape(token_count, HEADS * HEAD_DIM)))
        residual = resid + low_back(jnp.dot(attended, low(output_full), precision=HIGHEST, preferred_element_type=jnp.float32))
        normed_second = residual * lax.rsqrt(lax.optimization_barrier(jnp.mean(residual * residual, axis=-1, keepdims=True)) + NORM_EPSILON)
        scaled_second = low(normed_second * gains_low[1])
        gate_pre = low_back(jnp.dot(scaled_second, low(gate_full), precision=HIGHEST, preferred_element_type=jnp.float32))
        up_pre = low_back(jnp.dot(scaled_second, low(up_full), precision=HIGHEST, preferred_element_type=jnp.float32))
        hidden = low(jax.nn.silu(gate_pre) * up_pre)
        return residual + jnp.dot(hidden, low(down_full), precision=HIGHEST, preferred_element_type=jnp.float32)
    layouts = (True, False, False, False, True, True, False)
    masters = (query_weight, key_weight, value_weight, output_weight, gate_weight, up_weight, down_weight)
    full_weights = [to_full(master, rows_first) for master, rows_first in zip(masters, layouts)]
    resid_in = inputs.reshape(token_count, D).astype(jnp.float32)
    result, pullback = jax.vjp(forward_layer, resid_in, full_weights[0], full_weights[1], full_weights[2], full_weights[3], full_weights[4], full_weights[5], full_weights[6], norm_gains)
    gradients = pullback(cotangent.reshape(token_count, D).astype(jnp.float32))
    block_grads = [to_blocks(gradients[1 + number], layouts[number], masters[number].shape[1], masters[number].shape[2]) for number in range(7)]
    query_out = shampoo_step(block_grads[0], query_weight, query_left, query_right, query_leftroot, query_rightroot)
    key_out = shampoo_step(block_grads[1], key_weight, key_left, key_right, key_leftroot, key_rightroot)
    value_out = shampoo_step(block_grads[2], value_weight, value_left, value_right, value_leftroot, value_rightroot)
    output_out = shampoo_step(block_grads[3], output_weight, output_left, output_right, output_leftroot, output_rightroot)
    gate_out = shampoo_step(block_grads[4], gate_weight, gate_left, gate_right, gate_leftroot, gate_rightroot)
    up_out = shampoo_step(block_grads[5], up_weight, up_left, up_right, up_leftroot, up_rightroot)
    down_out = shampoo_step(block_grads[6], down_weight, down_left, down_right, down_leftroot, down_rightroot)
    gain_out = adam_step(gradients[8], norm_gains, gain_first, gain_second)
    block_out = result.reshape(ROWS, SEQ, D).astype(jnp.bfloat16)
    input_grad = gradients[0].reshape(ROWS, SEQ, D)
    return (block_out, input_grad, query_out[0], query_out[1], query_out[2], query_out[3], key_out[0], key_out[1], key_out[2], key_out[3], value_out[0], value_out[1], value_out[2], value_out[3], output_out[0], output_out[1], output_out[2], output_out[3], gate_out[0], gate_out[1], gate_out[2], gate_out[3], up_out[0], up_out[1], up_out[2], up_out[3], down_out[0], down_out[1], down_out[2], down_out[3], gain_out[0], gain_out[1], gain_out[2])
```

```python
import functools
import math

import jax
import jax.numpy as jnp
from jax import lax
from jax.experimental import pallas as pl
from jax.experimental.pallas import tpu as pltpu
from jax.sharding import PartitionSpec as P

HEADS = 32
KV_HEADS = 8
HEAD_DIM = 64
STEP = 10


NORM_EPSILON = 1e-05
ROPE_THETA = 500000.0
ROPE_FACTOR = 32.0
LOW_FACTOR = 1.0
HIGH_FACTOR = 4.0
BASE_SPAN = 8192.0
SCORE_SCALE = 0.125
MASKED = -1e30
SHAMPOO_DECAY = 0.95
SHAMPOO_RATE = 0.5
ADAM_RATE = 1.0
ADAM_FIRST = 0.9
ADAM_SECOND = 0.95
ADAM_EPSILON = 1e-08
QUERY_ROWS = 256
KEY_ROWS = 512
FEED_TILE = 512
BF16 = jnp.bfloat16
F32 = jnp.float32


def rope_rates():
    exponents = jnp.arange(0, HEAD_DIM, 2).astype(jnp.float32) / HEAD_DIM
    base_rates = 1.0 / ROPE_THETA**exponents
    wavelength = 2.0 * math.pi / base_rates
    smooth = (BASE_SPAN / wavelength - LOW_FACTOR) / (HIGH_FACTOR - LOW_FACTOR)
    blended = (1.0 - smooth) * base_rates / ROPE_FACTOR + smooth * base_rates
    longer = jnp.where(wavelength > BASE_SPAN / LOW_FACTOR, base_rates / ROPE_FACTOR, blended)
    return jnp.where(wavelength < BASE_SPAN / HIGH_FACTOR, base_rates, longer)


def adam_step(gradient, gains, first, second):
    first_new = ADAM_FIRST * first + (1.0 - ADAM_FIRST) * gradient
    second_new = ADAM_SECOND * second + (1.0 - ADAM_SECOND) * gradient * gradient
    corrected_first = first_new / (1.0 - ADAM_FIRST**STEP)
    corrected_second = second_new / (1.0 - ADAM_SECOND**STEP)
    return (
        first_new,
        second_new,
        gains - ADAM_RATE * corrected_first / (jnp.sqrt(corrected_second) + ADAM_EPSILON),
    )


def mul(left, right):
    return lax.dot_general(
        left, right, (((1,), (0,)), ((), ())), preferred_element_type=F32
    )


def mul_nt(left, right):
    return lax.dot_general(
        left, right, (((1,), (1,)), ((), ())), preferred_element_type=F32
    )


def mul_tn(left, right):
    return lax.dot_general(
        left, right, (((0,), (0,)), ((), ())), preferred_element_type=F32
    )


def turn(vectors, cos_table, sin_table):
    half = HEAD_DIM // 2
    former, latter = vectors[:half], vectors[half:]
    return jnp.concatenate(
        [former * cos_table - latter * sin_table, latter * cos_table + former * sin_table], axis=0
    )


def turn_back(vectors, cos_table, sin_table):
    return turn(vectors, cos_table, -sin_table)


def allowed_pairs(begins, query_block, key_block, query_rows, key_rows, copies):
    width = copies * query_rows
    key_index = key_block * key_rows + lax.broadcasted_iota(jnp.int32, (key_rows, width), 0)
    lane = lax.broadcasted_iota(jnp.int32, (1, query_rows), 1) + query_block * query_rows
    query_index = jnp.concatenate([lane] * copies, axis=1)
    begin_row = jnp.concatenate([begins] * copies, axis=1)
    return (key_index >= begin_row) & (key_index <= query_index)


def attend_kernel(
    copies,
    query_rows,
    key_rows,
    order_ref,
    first_ref,
    full_ref,
    begin_ref,
    qkv_ref,
    cos_ref,
    sin_ref,
    out_ref,
    query_ref,
    key_ref,
    keyt_ref,
    value_ref,
    lse_ref,
    valuet_ref,
):
    block = pl.program_id(0)
    width = copies * query_rows
    cos_table, sin_table = cos_ref[...], sin_ref[...]
    here = pl.ds(pl.multiple_of(block * query_rows, query_rows), query_rows)

    @pl.when(block == 0)
    def _():
        key_ref[...] = jnp.zeros_like(key_ref)
        keyt_ref[...] = jnp.zeros_like(keyt_ref)
        value_ref[...] = jnp.zeros_like(value_ref)
        valuet_ref[...] = jnp.zeros_like(valuet_ref)

    base = copies * HEAD_DIM
    keys = turn(qkv_ref[base : base + HEAD_DIM, :], cos_table, sin_table)
    values = qkv_ref[base + HEAD_DIM : base + 2 * HEAD_DIM, :]
    keyt_ref[:, here] = keys.astype(BF16)
    valuet_ref[:, here] = values.astype(BF16)
    key_ref[here, :] = keys.T.astype(BF16)
    value_ref[here, :] = values.T.astype(BF16)
    queries = jnp.concatenate(
        [
            turn(qkv_ref[h * HEAD_DIM : (h + 1) * HEAD_DIM, :], cos_table, sin_table)
            for h in range(copies)
        ],
        axis=1,
    ).astype(BF16) * jnp.asarray(SCORE_SCALE, BF16)
    query_ref[0] = queries
    begins = begin_ref[0]

    def visit(masked, number, state):
        peaks, totals, sums = state
        there = pl.ds(pl.multiple_of(number * key_rows, key_rows), key_rows)
        scores = mul(key_ref[there, :], queries)
        if masked:
            scores = jnp.where(
                allowed_pairs(begins, block, number, query_rows, key_rows, copies), scores, MASKED
            )
        new_peaks = jnp.maximum(peaks, jnp.max(scores, axis=0, keepdims=True))
        weights = jnp.exp(scores - new_peaks)
        factor = jnp.exp(peaks - new_peaks)
        totals = totals * factor + jnp.sum(weights, axis=0, keepdims=True)
        sums = sums * factor + mul(valuet_ref[:, there], weights.astype(BF16))
        return (new_peaks, totals, sums)

    state = (
        jnp.full((1, width), MASKED, F32),
        jnp.zeros((1, width), F32),
        jnp.zeros((HEAD_DIM, width), F32),
    )
    last = (block * query_rows) // key_rows
    first, full = first_ref[block], full_ref[block]
    state = lax.fori_loop(first, full, functools.partial(visit, True), state)
    state = lax.fori_loop(full, last, functools.partial(visit, False), state)
    peaks, totals, sums = visit(True, last, state)
    outs = (sums / totals).astype(BF16)
    for h in range(copies):
        out_ref[h * HEAD_DIM : (h + 1) * HEAD_DIM, :] = outs[:, h * query_rows : (h + 1) * query_rows]
    lse_ref[0] = peaks + jnp.log(totals)


def attend_back_kernel(
    copies,
    query_rows,
    key_rows,
    order_ref,
    first_ref,
    full_ref,
    begin_ref,
    query_ref,
    key_ref,
    keyt_ref,
    value_ref,
    lse_ref,
    out_ref,
    grad_ref,
    cos_ref,
    sin_ref,
    result_ref,
    dkey_ref,
    dvalue_ref,
):
    block = pl.program_id(0)
    width = copies * query_rows
    here = pl.ds(pl.multiple_of(block * query_rows, query_rows), query_rows)

    @pl.when(block == 0)
    def _():
        dkey_ref[...] = jnp.zeros_like(dkey_ref)
        dvalue_ref[...] = jnp.zeros_like(dvalue_ref)

    def place(number):
        return pl.ds(pl.multiple_of(order_ref[number] * query_rows, query_rows), query_rows)

    def spread(ref):
        return jnp.concatenate(
            [ref[h * HEAD_DIM : (h + 1) * HEAD_DIM, :] for h in range(copies)], axis=1
        )

    queries = query_ref[0]
    grads = spread(grad_ref)
    deltas = jnp.sum(grads.astype(F32) * spread(out_ref).astype(F32), axis=0, keepdims=True)
    lse = lse_ref[0]
    begins = begin_ref[0]

    def visit(masked, number, dquery):
        there = pl.ds(pl.multiple_of(number * key_rows, key_rows), key_rows)
        weights = jnp.exp(mul(key_ref[there, :], queries) - lse)
        if masked:
            weights = jnp.where(
                allowed_pairs(begins, block, number, query_rows, key_rows, copies), weights, 0.0
            )
        weight_grads = mul(value_ref[there, :], grads)
        score_grads = (weights * (weight_grads - deltas)).astype(BF16)
        dvalue_ref[there, :] += mul_nt(weights.astype(BF16), grads)
        dkey_ref[there, :] += mul_nt(score_grads, queries)
        return dquery + mul(keyt_ref[:, there], score_grads)

    last = (block * query_rows) // key_rows
    first, full = first_ref[block], full_ref[block]
    dquery = jnp.zeros((HEAD_DIM, width), F32)
    dquery = lax.fori_loop(first, full, functools.partial(visit, True), dquery)
    dquery = lax.fori_loop(full, last, functools.partial(visit, False), dquery)
    dquery = visit(True, last, dquery) * SCORE_SCALE
    cos_table, sin_table = cos_ref[:, here], sin_ref[:, here]
    for h in range(copies):
        piece = turn_back(dquery[:, h * query_rows : (h + 1) * query_rows], cos_table, sin_table)
        result_ref[h * HEAD_DIM : (h + 1) * HEAD_DIM, place(block)] = piece.astype(BF16)

    @pl.when(block == pl.num_programs(0) - 1)
    def _():
        base = copies * HEAD_DIM

        def finish(number, carried):
            rows = pl.ds(pl.multiple_of(number * query_rows, query_rows), query_rows)
            there = place(number)
            dkeys = turn_back(dkey_ref[rows, :].T, cos_ref[:, rows], sin_ref[:, rows])
            result_ref[base : base + HEAD_DIM, there] = dkeys.astype(BF16)
            dvalues = dvalue_ref[rows, :].T.astype(BF16)
            result_ref[base + HEAD_DIM : base + 2 * HEAD_DIM, there] = dvalues
            return carried

        lax.fori_loop(0, pl.num_programs(0), finish, 0)


def attend(qkv, cos_table, sin_table, begins, order, first, full, copies, query_rows, key_rows):
    total = qkv.shape[1]
    blocks = total // query_rows
    base = copies * HEAD_DIM
    width = copies * query_rows
    pairs = copies * total * total // 2
    return pl.pallas_call(
        functools.partial(attend_kernel, copies, query_rows, key_rows),
        grid_spec=pltpu.PrefetchScalarGridSpec(
        num_scalar_prefetch=3,
        grid=(blocks,),
        in_specs=[
            pl.BlockSpec((1, 1, query_rows), lambda i, order, first, full: (i, 0, 0)),
            pl.BlockSpec((base + 2 * HEAD_DIM, query_rows), lambda i, order, first, full: (0, order[i])),
            pl.BlockSpec((HEAD_DIM // 2, query_rows), lambda i, order, first, full: (0, i)),
            pl.BlockSpec((HEAD_DIM // 2, query_rows), lambda i, order, first, full: (0, i)),
        ],
        out_specs=[
            pl.BlockSpec((base, query_rows), lambda i, order, first, full: (0, order[i])),
            pl.BlockSpec((1, HEAD_DIM, width), lambda i, order, first, full: (i, 0, 0)),
            pl.BlockSpec((total, HEAD_DIM), lambda i, order, first, full: (0, 0)),
            pl.BlockSpec((HEAD_DIM, total), lambda i, order, first, full: (0, 0)),
            pl.BlockSpec((total, HEAD_DIM), lambda i, order, first, full: (0, 0)),
            pl.BlockSpec((1, 1, width), lambda i, order, first, full: (i, 0, 0)),
        ],
        scratch_shapes=[pltpu.VMEM((HEAD_DIM, total), BF16)],
        ),
        out_shape=[
            jax.ShapeDtypeStruct((base, total), BF16),
            jax.ShapeDtypeStruct((blocks, HEAD_DIM, width), BF16),
            jax.ShapeDtypeStruct((total, HEAD_DIM), BF16),
            jax.ShapeDtypeStruct((HEAD_DIM, total), BF16),
            jax.ShapeDtypeStruct((total, HEAD_DIM), BF16),
            jax.ShapeDtypeStruct((blocks, 1, width), F32),
        ],
        compiler_params=pltpu.CompilerParams(
            dimension_semantics=("arbitrary",), vmem_limit_bytes=48 * 1024 * 1024
        ),
        cost_estimate=pl.CostEstimate(
            flops=4 * pairs * HEAD_DIM, bytes_accessed=8 * 1024 * 1024, transcendentals=pairs
        ),
        name="attend",
    )(order, first, full, begins, qkv, cos_table, sin_table)


def attend_back(
    saved, grads, cos_table, sin_table, begins, order, first, full, copies, query_rows, key_rows
):
    out, queries, keys, keys_t, values, lse = saved
    total = keys.shape[0]
    blocks = total // query_rows
    base = copies * HEAD_DIM
    width = copies * query_rows
    pairs = copies * total * total // 2
    whole = lambda i, order, first, full: (0, 0)
    return pl.pallas_call(
        functools.partial(attend_back_kernel, copies, query_rows, key_rows),
        grid_spec=pltpu.PrefetchScalarGridSpec(
        num_scalar_prefetch=3,
        grid=(blocks,),
        in_specs=[
            pl.BlockSpec((1, 1, query_rows), lambda i, order, first, full: (i, 0, 0)),
            pl.BlockSpec((1, HEAD_DIM, width), lambda i, order, first, full: (i, 0, 0)),
            pl.BlockSpec((total, HEAD_DIM), whole),
            pl.BlockSpec((HEAD_DIM, total), whole),
            pl.BlockSpec((total, HEAD_DIM), whole),
            pl.BlockSpec((1, 1, width), lambda i, order, first, full: (i, 0, 0)),
            pl.BlockSpec((base, query_rows), lambda i, order, first, full: (0, order[i])),
            pl.BlockSpec((base, query_rows), lambda i, order, first, full: (0, order[i])),
            pl.BlockSpec((HEAD_DIM // 2, total), whole),
            pl.BlockSpec((HEAD_DIM // 2, total), whole),
        ],
        out_specs=pl.BlockSpec((base + 2 * HEAD_DIM, total), whole),
        scratch_shapes=[
            pltpu.VMEM((total, HEAD_DIM), F32),
            pltpu.VMEM((total, HEAD_DIM), F32),
        ],
        ),
        out_shape=jax.ShapeDtypeStruct((base + 2 * HEAD_DIM, total), BF16),
        compiler_params=pltpu.CompilerParams(
            dimension_semantics=("arbitrary",), vmem_limit_bytes=48 * 1024 * 1024
        ),
        cost_estimate=pl.CostEstimate(
            flops=10 * pairs * HEAD_DIM, bytes_accessed=8 * 1024 * 1024, transcendentals=pairs
        ),
        name="attend_back",
    )(
        order, first, full, begins, queries, keys, keys_t, values, lse, out, grads, cos_table, sin_table
    )


def norm(rows):
    inverse = lax.rsqrt(jnp.mean(rows * rows, axis=-1, keepdims=True) + NORM_EPSILON)
    return rows * inverse, inverse


def norm_back(gradient, normed, inverse):
    return inverse * (gradient - normed * jnp.mean(gradient * normed, axis=-1, keepdims=True))


def project_kernel(gains_ref, weight_ref, own_ref, other_ref, *refs):
    scaled_ref, result_ref = refs[-2:]
    rows = own_ref.shape[0]
    for half, ref in enumerate((own_ref, other_ref)):
        chunk = ref[...].astype(F32)
        inverse = lax.rsqrt(jnp.mean(chunk * chunk, axis=-1, keepdims=True) + NORM_EPSILON)
        scaled = (chunk * inverse * gains_ref[...]).astype(BF16)
        scaled_ref[0, half * rows : (half + 1) * rows, :] = scaled
        result_ref[:, half * rows : (half + 1) * rows] = mul_nt(weight_ref[...], scaled)


def project(step, places, gains, weight, own, other, held):
    rows, width = own.shape
    outputs = weight.shape[0]
    whole = lambda i: (0, 0)
    return pl.pallas_call(
        project_kernel,
        grid=(1,),
        in_specs=[
            pl.BlockSpec((1, width), whole),
            pl.BlockSpec((outputs, width), whole),
            pl.BlockSpec((rows, width), whole),
            pl.BlockSpec((rows, width), whole),
        ]
        + [pl.BlockSpec(memory_space=pl.ANY)] * len(held),
        out_specs=[
            pl.BlockSpec((1, 2 * rows, width), lambda i: (step, 0, 0)),
            pl.BlockSpec((outputs, 2 * rows), lambda i: (0, step)),
        ],
        out_shape=[
            jax.ShapeDtypeStruct((places, 2 * rows, width), BF16),
            jax.ShapeDtypeStruct((outputs, places * 2 * rows), F32),
        ],
        input_output_aliases={4 + n: n for n in range(len(held))},
        compiler_params=pltpu.CompilerParams(vmem_limit_bytes=48 * 1024 * 1024),
        cost_estimate=pl.CostEstimate(
            flops=4 * rows * width * outputs, bytes_accessed=8 * rows * width, transcendentals=0
        ),
        name="project",
    )(gains, weight, own, other, *held)


def feed_kernel(
    row_parts, where_ref, own_ref, other_ref, grad_own_ref, grad_other_ref, *refs
):
    gate_refs, up_refs, down_refs = [
        refs[n * row_parts : (n + 1) * row_parts] for n in range(3)
    ]
    (
        scaled_ref,
        upstream_ref,
        hidden_ref,
        gate_low_ref,
        up_low_ref,
        back_own_ref,
        back_other_ref,
        out_own_ref,
        out_other_ref,
        back_ref,
        out_ref,
    ) = refs[-11:]
    step = pl.program_id(0)
    rows = own_ref.shape[0]
    size = down_refs[0].shape[1]

    @pl.when(step == 0)
    def _():
        scaled_ref[0, :rows, :] = own_ref[...]
        scaled_ref[0, rows:, :] = other_ref[...]
        upstream_ref[0, :rows, :] = grad_own_ref[...]
        upstream_ref[0, rows:, :] = grad_other_ref[...]
        out_ref[...] = jnp.zeros_like(out_ref)
        back_ref[...] = jnp.zeros_like(back_ref)

    places = [
        pl.ds(pl.multiple_of(where_ref[part] * size, size), size) for part in range(row_parts)
    ]
    gate_pre = up_pre = hidden_grad = 0.0
    for part, here in enumerate(places):
        scaled = scaled_ref[0, :, here]
        gate_pre += mul(scaled, gate_refs[part][...])
        up_pre += mul(scaled, up_refs[part][...])
        hidden_grad += mul_nt(upstream_ref[0, :, here], down_refs[part][...])
    sigmoid_gate = 1.0 / (1.0 + jnp.exp(-gate_pre))
    silu_gate = gate_pre * sigmoid_gate
    hidden = (silu_gate * up_pre).astype(BF16)
    gate_low = (hidden_grad * up_pre * sigmoid_gate * (1.0 + gate_pre * (1.0 - sigmoid_gate))).astype(
        BF16
    )
    up_low = (hidden_grad * silu_gate).astype(BF16)
    hidden_ref[0] = hidden
    gate_low_ref[0] = gate_low
    up_low_ref[0] = up_low
    both_low = jnp.concatenate([gate_low, up_low], axis=1)
    for part, here in enumerate(places):
        out_ref[:, here] += mul(hidden, down_refs[part][...])
        both = jnp.concatenate([gate_refs[part][...], up_refs[part][...]], axis=1)
        back_ref[:, here] += mul_nt(both_low, both)

    @pl.when(step == pl.num_programs(0) - 1)
    def _():
        back_own_ref[...] = back_ref[:rows, :].astype(BF16)
        back_other_ref[...] = back_ref[rows:, :].astype(BF16)
        out_own_ref[...] = out_ref[:rows, :].astype(BF16)
        out_other_ref[...] = out_ref[rows:, :].astype(BF16)


def feed(step, places, where, own, other, grad_own, grad_other, weights, held):
    rows, width = own.shape
    row_parts = len(weights[0])
    size, inner = weights[1][0].shape
    tile = min(FEED_TILE, inner, size)
    tall = size // tile
    shard = pl.BlockSpec((rows, width), lambda i, where: (0, 0))
    gate = pl.BlockSpec((size, tile), lambda i, where: (0, i))
    down = pl.BlockSpec((tile, size), lambda i, where: (i % tall, i // tall))
    kept = pl.BlockSpec((1, 2 * rows, width), lambda i, where: (step, 0, 0))
    kept_inner = pl.BlockSpec((1, 2 * rows, tile), lambda i, where: (step, 0, i))
    return pl.pallas_call(
        functools.partial(feed_kernel, row_parts),
        grid_spec=pltpu.PrefetchScalarGridSpec(
            num_scalar_prefetch=1,
            grid=(inner // tile,),
            in_specs=[shard] * 4
            + [gate] * (2 * row_parts)
            + [down] * row_parts
            + [pl.BlockSpec(memory_space=pl.ANY)] * len(held),
            out_specs=[kept] * 2
            + [kept_inner] * 3
            + [shard] * 4,
            scratch_shapes=[pltpu.VMEM((2 * rows, width), F32)] * 2,
        ),
        out_shape=[jax.ShapeDtypeStruct((places, 2 * rows, width), BF16)] * 2
        + [jax.ShapeDtypeStruct((places, 2 * rows, inner), BF16)] * 3
        + [jax.ShapeDtypeStruct((rows, width), BF16)] * 4,
        input_output_aliases={5 + 3 * row_parts + n: n for n in range(len(held))},
        compiler_params=pltpu.CompilerParams(
            dimension_semantics=("arbitrary",), vmem_limit_bytes=60 * 1024 * 1024
        ),
        cost_estimate=pl.CostEstimate(
            flops=24 * rows * width * inner,
            bytes_accessed=32 * rows * width + 6 * width * inner,
            transcendentals=2 * rows * inner,
        ),
        name="feed",
    )(
        where, own, other, grad_own, grad_other, *weights[0], *weights[1], *weights[2], *held
    )


def split_kernel(base, where_ref, entry_ref, send_ref):
    blocks, rows, _ = send_ref.shape
    key_in = rows - 16
    key_out = entry_ref.shape[2] - base
    per_row = key_out // HEAD_DIM
    shares = blocks // KV_HEADS
    line = lax.broadcasted_iota(jnp.int32, (16, 2 * HEAD_DIM), 0)
    gains = jnp.zeros((16, 2 * HEAD_DIM), F32)
    for part in range(entry_ref.shape[0]):
        here = where_ref[part]
        top = entry_ref[here, 2 * key_in : 2 * key_in + 16, : 2 * HEAD_DIM].astype(F32)
        gains = jnp.where(line == part, top[:1], gains)
    for head in range(KV_HEADS):
        here = where_ref[head // per_row]
        start = base + head % per_row * HEAD_DIM
        piece = jnp.concatenate(
            [
                entry_ref[here, :key_in, start : start + HEAD_DIM],
                entry_ref[here, key_in : 2 * key_in, start : start + HEAD_DIM],
            ],
            axis=1,
        )
        for number in range(head * shares, (head + 1) * shares):
            send_ref[number, :key_in, :] = piece
            send_ref[number, key_in:, :] = gains.astype(BF16)


def split_entry(where, entry, base, blocks, key_in):
    return pl.pallas_call(
        functools.partial(split_kernel, base),
        grid_spec=pltpu.PrefetchScalarGridSpec(
            num_scalar_prefetch=1,
            grid=(1,),
            in_specs=[pl.BlockSpec(entry.shape, lambda i, where: (0, 0, 0))],
            out_specs=pl.BlockSpec(
                (blocks, key_in + 16, 2 * HEAD_DIM), lambda i, where: (0, 0, 0)
            ),
        ),
        out_shape=jax.ShapeDtypeStruct((blocks, key_in + 16, 2 * HEAD_DIM), BF16),
        name="split_entry",
    )(where, entry)


def join_kernel(base, where_ref, entry_ref, kv_ref, plain_ref, turned_ref):
    blocks, rows, depth = kv_ref.shape
    key_in = rows - 16
    size = entry_ref.shape[1] - 16
    for part in range(entry_ref.shape[0]):
        block = entry_ref[where_ref[part], :size, :base]
        here = slice(part * size, (part + 1) * size)
        plain_ref[here, :base] = block
        turned_ref[:base, here] = block.astype(F32).T.astype(BF16)
    for number in range(blocks):
        block = kv_ref[number, :key_in, :]
        here = slice(number * key_in, (number + 1) * key_in)
        plain_ref[here, base:] = block
        turned_ref[base:, here] = block.astype(F32).T.astype(BF16)


def join_weights(where, entry, kv, base, width):
    depth = base + 2 * HEAD_DIM
    return pl.pallas_call(
        functools.partial(join_kernel, base),
        grid_spec=pltpu.PrefetchScalarGridSpec(
            num_scalar_prefetch=1,
            grid=(1,),
            in_specs=[
                pl.BlockSpec(entry.shape, lambda i, where: (0, 0, 0)),
                pl.BlockSpec(kv.shape, lambda i, where: (0, 0, 0)),
            ],
            out_specs=[
                pl.BlockSpec((width, depth), lambda i, where: (0, 0)),
                pl.BlockSpec((depth, width), lambda i, where: (0, 0)),
            ],
        ),
        out_shape=[
            jax.ShapeDtypeStruct((width, depth), BF16),
            jax.ShapeDtypeStruct((depth, width), BF16),
        ],
        name="join_weights",
    )(where, entry, kv)


def projection_grad_kernel(base, grads_ref, scaled_ref, weight_ref, query_ref, kv_ref, gain_ref):
    product = mul(grads_ref[...], scaled_ref[...])
    gain_ref[...] = jnp.sum(product * weight_ref[...].astype(F32), axis=0, keepdims=True)
    query_ref[0] = product[:base].T.astype(BF16)
    count, size, _ = kv_ref.shape
    for number in range(count):
        kv_ref[number] = product[base:, number * size : (number + 1) * size].T.astype(BF16)


def projection_grad(grads, scaled, weight, base, row_parts, block_parts):
    depth, total = grads.shape
    width = scaled.shape[1]
    size, key_in = width // row_parts, width // block_parts
    count = block_parts // row_parts
    return pl.pallas_call(
        functools.partial(projection_grad_kernel, base),
        grid=(row_parts,),
        in_specs=[
            pl.BlockSpec((depth, total), lambda i: (0, 0)),
            pl.BlockSpec((total, size), lambda i: (0, i)),
            pl.BlockSpec((depth, size), lambda i: (0, i)),
        ],
        out_specs=[
            pl.BlockSpec((1, size, base), lambda i: (i, 0, 0)),
            pl.BlockSpec((count, key_in, depth - base), lambda i: (i, 0, 0)),
            pl.BlockSpec((1, size), lambda i: (0, i)),
        ],
        out_shape=[
            jax.ShapeDtypeStruct((row_parts, size, base), BF16),
            jax.ShapeDtypeStruct((block_parts, key_in, depth - base), BF16),
            jax.ShapeDtypeStruct((1, width), F32),
        ],
        compiler_params=pltpu.CompilerParams(
            dimension_semantics=("arbitrary",), vmem_limit_bytes=48 * 1024 * 1024
        ),
        cost_estimate=pl.CostEstimate(
            flops=2 * depth * total * width, bytes_accessed=2 * total * width, transcendentals=0
        ),
        name="projection_grad",
    )(grads, scaled, weight)


def shampoo_kernel(
    gradient_ref,
    columns_ref,
    master_ref,
    left_ref,
    right_ref,
    left_root_ref,
    right_root_ref,
    wide_ref,
    new_ref,
    left_new_ref,
    right_new_ref,
):
    rows = master_ref.shape[1]
    here = pl.ds(pl.multiple_of(pl.program_id(0) * rows, rows), rows)
    gradient = gradient_ref[...].astype(BF16)
    mine = gradient_ref[here, :].astype(F32)
    wide_ref[0] = mine
    left = mul_nt(mine.astype(BF16), gradient)
    left_new_ref[0] = SHAMPOO_DECAY * left_ref[0] + (1.0 - SHAMPOO_DECAY) * left
    turned = columns_ref[...].astype(F32).T.astype(BF16)
    right = mul(turned, gradient)
    right_new_ref[0] = SHAMPOO_DECAY * right_ref[0] + (1.0 - SHAMPOO_DECAY) * right
    half = mul(left_root_ref[0].astype(BF16), gradient).astype(BF16)
    direction = mul(half, right_root_ref[0].astype(BF16))
    new_ref[0] = master_ref[0] - SHAMPOO_RATE * direction


def shampoo(gradient, master, left, right, left_root, right_root):
    rows, columns = gradient.shape
    steps = max(1, min(4, columns // 128))
    tile, wide = rows // steps, columns // steps

    def lines(height, width):
        return pl.BlockSpec((1, height, width), lambda i: (0, i, 0))

    return pl.pallas_call(
        shampoo_kernel,
        grid=(steps,),
        in_specs=[
            pl.BlockSpec((rows, columns), lambda i: (0, 0)),
            pl.BlockSpec((rows, wide), lambda i: (0, i)),
            lines(tile, columns),
            lines(tile, rows),
            lines(wide, columns),
            lines(tile, rows),
            pl.BlockSpec((1, columns, columns), lambda i: (0, 0, 0)),
        ],
        out_specs=[lines(tile, columns)] * 2 + [lines(tile, rows), lines(wide, columns)],
        out_shape=[jax.ShapeDtypeStruct(master.shape, F32)] * 2
        + [jax.ShapeDtypeStruct(left.shape, F32), jax.ShapeDtypeStruct(right.shape, F32)],
        compiler_params=pltpu.CompilerParams(
            dimension_semantics=("arbitrary",), vmem_limit_bytes=48 * 1024 * 1024
        ),
        cost_estimate=pl.CostEstimate(
            flops=4 * rows * columns * (rows + columns),
            bytes_accessed=12 * (rows * rows + columns * columns + rows * columns),
            transcendentals=0,
        ),
        name="shampoo",
    )(gradient, gradient, master, left, right, left_root, right_root)


def arrange_kernel(width, where_ref, *refs):
    result_ref = refs[-1]
    count, wide = refs[0].shape
    for part, ref in enumerate(refs[:-1]):
        here = pl.ds(pl.multiple_of(where_ref[part] * width, width), width)
        for piece in range(wide // width):
            rows = slice(piece * count, (piece + 1) * count)
            result_ref[rows, here] = ref[:, piece * width : (piece + 1) * width]


def arrange_output(where, items, start, base, width):
    count = items[0].shape[0] - start
    wide = items[0].shape[1]
    row_parts = len(items)
    return pl.pallas_call(
        functools.partial(arrange_kernel, width // row_parts),
        grid_spec=pltpu.PrefetchScalarGridSpec(
            num_scalar_prefetch=1,
            grid=(1,),
            in_specs=[
                pl.BlockSpec((count, wide), lambda i, where: (start // count, 0))
            ]
            * row_parts,
            out_specs=pl.BlockSpec((base, width), lambda i, where: (0, 0)),
        ),
        out_shape=jax.ShapeDtypeStruct((base, width), BF16),
        name="arrange_output",
    )(where, *items)


def down_grad_kernel(hidden_ref, upstream_ref, result_ref, turned_ref):
    rows = 256

    @pl.when(pl.program_id(0) == 0)
    def _():
        def turn_rows(number, carried):
            here = pl.ds(pl.multiple_of(number * rows, rows), rows)
            turned_ref[:, here] = hidden_ref[here, :].astype(F32).T.astype(BF16)
            return carried

        lax.fori_loop(0, hidden_ref.shape[0] // rows, turn_rows, 0)

    result_ref[0] = mul(turned_ref[...], upstream_ref[...]).astype(BF16)


def down_gradient(hidden, upstream, row_parts):
    total, inner = hidden.shape
    width = upstream.shape[1]
    size = width // row_parts
    return pl.pallas_call(
        down_grad_kernel,
        grid=(row_parts,),
        in_specs=[
            pl.BlockSpec((total, inner), lambda i: (0, 0)),
            pl.BlockSpec((total, size), lambda i: (0, i)),
        ],
        out_specs=pl.BlockSpec((1, inner, size), lambda i: (i, 0, 0)),
        out_shape=jax.ShapeDtypeStruct((row_parts, inner, size), BF16),
        scratch_shapes=[pltpu.VMEM((inner, total), BF16)],
        compiler_params=pltpu.CompilerParams(
            dimension_semantics=("arbitrary",), vmem_limit_bytes=48 * 1024 * 1024
        ),
        cost_estimate=pl.CostEstimate(
            flops=2 * total * inner * width,
            bytes_accessed=2 * total * (inner + width),
            transcendentals=0,
        ),
        name="down_gradient",
    )(hidden, upstream)


def spread_kernel(rows_ref, weight_ref, *out_refs):
    block = pl.program_id(0)
    part = mul(rows_ref[...].astype(F32).T.astype(BF16), weight_ref[...]).astype(BF16)
    for number, ref in enumerate(out_refs):

        @pl.when(block == number)
        def _():
            ref[...] = part


def spread_parts(rows, weight, blocks):
    depth, total = rows.shape
    width = weight.shape[1]
    count = total // blocks
    shard = pl.BlockSpec((count, width), lambda i: (0, 0))
    return pl.pallas_call(
        spread_kernel,
        grid=(blocks,),
        in_specs=[
            pl.BlockSpec((depth, count), lambda i: (0, i)),
            pl.BlockSpec((depth, width), lambda i: (0, 0)),
        ],
        out_specs=[shard] * blocks,
        out_shape=[jax.ShapeDtypeStruct((count, width), BF16)] * blocks,
        compiler_params=pltpu.CompilerParams(
            dimension_semantics=("arbitrary",), vmem_limit_bytes=48 * 1024 * 1024
        ),
        cost_estimate=pl.CostEstimate(
            flops=2 * depth * total * width,
            bytes_accessed=2 * total * width,
            transcendentals=0,
        ),
        name="spread",
    )(rows, weight)


def output_back_kernel(columns, weight_ref, attended_ref, *refs):
    shard_refs, out_grad_ref, weight_grad_ref = refs[:-2], refs[-2], refs[-1]
    count = shard_refs[0].shape[0]
    total = None
    for number, ref in enumerate(shard_refs):
        shard = ref[...]
        here = slice(number * count, (number + 1) * count)
        out_grad_ref[:, here] = mul_nt(weight_ref[...], shard).astype(BF16)
        part = mul(attended_ref[:, here], shard)
        total = part if total is None else total + part
    for piece in range(weight_grad_ref.shape[0]):
        weight_grad_ref[piece] = total[:, piece * columns : (piece + 1) * columns].astype(BF16)


def output_back(weight, attended, shards_all, row_parts):
    depth, width = weight.shape
    total = attended.shape[1]
    columns = width // row_parts
    whole = lambda i: (0, 0)
    return pl.pallas_call(
        functools.partial(output_back_kernel, columns),
        grid=(1,),
        in_specs=[pl.BlockSpec((depth, width), whole), pl.BlockSpec((depth, total), whole)]
        + [pl.BlockSpec(item.shape, whole) for item in shards_all],
        out_specs=[
            pl.BlockSpec((depth, total), whole),
            pl.BlockSpec((row_parts, depth, columns), lambda i: (0, 0, 0)),
        ],
        out_shape=[
            jax.ShapeDtypeStruct((depth, total), BF16),
            jax.ShapeDtypeStruct((row_parts, depth, columns), BF16),
        ],
        compiler_params=pltpu.CompilerParams(vmem_limit_bytes=52 * 1024 * 1024),
        cost_estimate=pl.CostEstimate(
            flops=4 * depth * total * width, bytes_accessed=2 * total * width, transcendentals=0
        ),
        name="output_back",
    )(weight, attended, *shards_all)


def together(*values):
    return lax.optimization_barrier(values)


def after(value, *others):
    return lax.optimization_barrier((value,) + others)[0]


def send(array, pairs):
    both = [(2 * here + core, 2 * there + core) for here, there in pairs for core in range(2)]
    return lax.ppermute(array, "blk", both)


def row_send(array, row_parts, flip):
    return lax.ppermute(array, "row", [(n, n ^ flip) for n in range(row_parts)])


def row_sends(block, row_parts, flips=None):
    return [row_send(block, row_parts, flip) for flip in (flips or range(1, row_parts))]


def row_exchange(pieces):
    me = lax.axis_index("row")
    items = [
        lax.dynamic_index_in_dim(pieces, me ^ flip, 0, False) for flip in range(len(pieces))
    ]
    return [items[0]] + [row_send(items[n], len(items), n) for n in range(1, len(items))]


def row_sum(items):
    return sum(item.astype(F32) for item in items)


def shards(*arguments):
    (inputs, cotangent, doc_lengths, norm_gains, gain_first, gain_second) = arguments[:6]
    state = [arguments[6 + 5 * n : 11 + 5 * n] for n in range(7)]
    query_weight, key_weight, value_weight, output_weight, gate_weight, up_weight, down_weight = [
        group[0][0] for group in state
    ]
    row_parts = lax.axis_size("row")
    block_parts = lax.axis_size("blk")
    devices = row_parts * block_parts
    places = block_parts // 2
    copies = HEADS // block_parts
    shares = block_parts // KV_HEADS
    token_count = inputs.shape[1]
    total = token_count * block_parts
    width = inputs.shape[2]
    base = copies * HEAD_DIM
    gain_width = norm_gains.shape[1]
    key_in, key_out = key_weight.shape
    query_in = query_weight.shape[0]
    inner = gate_weight.shape[1]
    me = lax.axis_index("blk")
    place = me // 2
    upward = [(n, (n + 1) % places) for n in range(places)]
    downward = [(n, (n - 1) % places) for n in range(places)]
    head_pair = 2 * HEAD_DIM
    spare = 16

    def low(array):
        return array.astype(BF16)

    def pad_to(array, rows, columns):
        return jnp.pad(array, ((0, rows - array.shape[0]), (0, columns - array.shape[1])))

    def swapped(array):
        return lax.ppermute(array, "blk", [(n, n ^ 1) for n in range(block_parts)])

    where = lax.axis_index("row") ^ jnp.arange(row_parts, dtype=jnp.int32)
    down_wide = down_weight.reshape(inner // query_in, query_in, query_in).transpose(1, 0, 2)
    down_wide = down_wide.reshape(query_in, inner)
    half_flips = list(range(1, row_parts - 1)), [row_parts - 1]

    shard = inputs[0]
    entry = jnp.concatenate([low(query_weight), low(jnp.concatenate([key_weight, value_weight]))], 1)
    gain_line = low(norm_gains).reshape(1, 2 * gain_width)
    entry = jnp.concatenate([entry, pad_to(gain_line, spare, entry.shape[1])], axis=0)
    tokens = [shard, send(shard, upward)]
    pieces = inner // output_weight.shape[1]
    output_wide = jnp.concatenate(jnp.split(low(output_weight), pieces, axis=0), axis=1)
    tokens[1], gate_low, *entries = together(
        tokens[1],
        jnp.concatenate([low(gate_weight), output_wide], axis=0),
        *row_sends(entry, row_parts),
    )
    entry = jnp.stack([entry, *entries])
    kv_send = split_entry(where, entry, base, block_parts, key_in)
    token_others = [swapped(shard)]
    following = send(tokens[1], upward)
    following, kv_slice, entry, down_low, up_low_weight, *gate_items = together(
        following,
        lax.all_to_all(kv_send, "blk", 0, 0),
        entry,
        low(down_wide),
        low(up_weight),
        *row_sends(gate_low, row_parts, half_flips[0]),
    )
    tokens.append(following)
    qkv_full, qkv_turned = join_weights(where, entry, kv_slice, base, width)
    gains = kv_slice[:, key_in : key_in + row_parts, : 2 * gain_width]
    gains = gains.reshape(block_parts, row_parts, 2, gain_width).transpose(2, 1, 0, 3)
    gains = gains.reshape(2, 1, width).astype(F32)
    token_others.append(swapped(tokens[1]))
    while len(tokens) < places:
        tokens.append(send(tokens[-1], upward))
        token_others.append(swapped(tokens[-2]))
    count = len(tokens)
    qkv_turned, gains, up_low_weight, *released = together(
        qkv_turned,
        gains,
        up_low_weight,
        cotangent[0],
        *tokens,
        *token_others,
        *row_sends(gate_low, row_parts, half_flips[1]),
    )
    upstream = [released[0]]
    tokens, token_others = released[1 : 1 + count], list(released[1 + count : 2 * count])
    gate_items = [gate_low, *gate_items, *released[2 * count :]]
    output_full = arrange_output(where, gate_items, query_in, base, width)

    lengths_row = doc_lengths[0]
    doc_ends = jnp.cumsum(lengths_row)
    doc_starts = doc_ends - lengths_row
    positions = jnp.arange(total, dtype=jnp.int32)
    inside = (positions[:, None] >= doc_starts[None, :]) & (positions[:, None] < doc_ends[None, :])
    begins = jnp.sum(jnp.where(inside, doc_starts[None, :], 0), axis=-1)
    angles = rope_rates()[:, None] * (positions - begins).astype(F32)[None, :]
    cos_table, sin_table = jnp.cos(angles), jnp.sin(angles)
    begin_rows = begins.reshape(block_parts, 1, token_count)
    key_rows = 2 * token_count
    last_block = (jnp.arange(block_parts, dtype=jnp.int32) * token_count) // key_rows
    first = begin_rows[:, 0, 0] // key_rows
    full = jnp.clip((begin_rows[:, 0, -1] + key_rows - 1) // key_rows, first, last_block)
    numbers = jnp.arange(block_parts, dtype=jnp.int32)
    order = 2 * ((place - numbers // 2) % places) + (numbers % 2 != me % 2)
    layout = (cos_table, sin_table, begin_rows, order.astype(jnp.int32), first, full)
    sizes = (copies, token_count, key_rows)

    token_others.append(swapped(tokens[-1]))
    held = ()
    for step in range(places):
        held = project(
            step, places, gains[0], qkv_turned, tokens[step], token_others[step], held
        )
    upstream.append(send(upstream[-1], upward))
    upstream[-1], qkv, scaled_first, output_full, *up_items = together(
        upstream[-1],
        held[1],
        held[0],
        output_full,
        *row_sends(up_low_weight, row_parts, half_flips[0]),
    )
    scaled_first = scaled_first.reshape(total, width)
    following = send(upstream[-1], upward)
    saved = attend(qkv, *layout, *sizes)
    following, attended, *last_items = together(
        following, saved[0], *row_sends(up_low_weight, row_parts, half_flips[1])
    )
    upstream.append(following)
    up_items = [up_low_weight, *up_items, *last_items]

    def pair_sums(own_parts, other_parts):
        return [
            low(own.astype(F32) + swapped(other).astype(F32))
            for own, other in zip(own_parts, other_parts)
        ]

    parts = spread_parts(attended, output_full, block_parts)
    while len(upstream) < places:
        upstream.append(send(upstream[-1], upward))
    released = together(*parts, *upstream)
    own_parts, other_parts = released[0 : 2 * places : 2], released[1 : 2 * places : 2]
    upstream = released[2 * places :]
    part, = together(*pair_sums(own_parts[1:2], other_parts[1:2]))
    upstream_others, down_items = [], [down_low]
    for step in range(2, places + 1):
        work = []
        if step == 2:
            work = [
                *pair_sums(own_parts[2:], other_parts[2:]),
                *pair_sums(own_parts[:1], other_parts[:1]),
            ]
        elif step == 3:
            work = [
                *row_sends(down_low, row_parts, half_flips[0]),
                *[swapped(item) for item in upstream[:2]],
            ]
        elif step == 4:
            work = [
                *row_sends(down_low, row_parts, half_flips[1]),
                *[swapped(item) for item in upstream[2:]],
            ]
        arrived, *work = together(send(part, upward), *work)
        if step == 2:
            parts = [work[-1], None, *work[:-1]]
        elif step == 3:
            down_items += work[:-2]
            upstream_others += work[-2:]
        elif step == 4:
            down_items.append(work[0])
            upstream_others += work[1:]
        added = parts[step % places].astype(F32) + arrived.astype(F32)
        part = low(added)
    resid = inputs[0].astype(F32)
    residual = resid + added
    normed_second, inverse_second = norm(residual)

    own = low(normed_second * gains[1])
    own, other = together(own, swapped(own))
    held = ()
    part = carried = None
    result_own, result_other = [], []
    for step in range(places):
        following = send(own, upward) if step + 1 < places else own
        if part is not None:
            carried = send(part, upward)
        outs = feed(
            step,
            places,
            where,
            own,
            other,
            upstream[step],
            upstream_others[step],
            (gate_items, up_items, down_items),
            held,
        )
        held = outs[:5]
        result_own.append(outs[7])
        result_other.append(outs[8])
        released = [following, *outs[5:7]] + ([carried] if part is not None else [])
        released = together(*released)
        own = released[0]
        back_own, back_other = released[1:3]
        fresh = swapped(own) if step + 1 < places else other
        if step == 0:
            last_own, last_other = back_own, back_other
            own, other = together(own, fresh)
        else:
            added = back_own.astype(F32) + swapped(back_other).astype(F32)
            if part is not None:
                added = added + released[3].astype(F32)
            own, other, part = together(own, fresh, low(added))
    second_all, upstream_all, hidden_all, gate_low_all, up_low_all = [
        item.reshape(total, item.shape[2]) for item in held
    ]

    def split_rows(grad):
        size_in, size_out = grad.shape
        return low(grad).reshape(row_parts, size_in // row_parts, size_out)

    def scatter(split):
        return lax.psum_scatter(split, "row", scatter_dimension=0, tiled=True)[0]

    def update(group, gradient):
        return shampoo(gradient, *group)


    carried = send(part, upward)
    last_other = swapped(last_other)
    gate_grad = split_rows(mul_tn(after(second_all, part), gate_low_all))
    carried, last_own, last_other, gate_grad = together(carried, last_own, last_other, gate_grad)
    gate_sum = scatter(gate_grad)
    second_grad = last_own.astype(F32) + last_other.astype(F32) + carried.astype(F32)
    residual_grad = cotangent[0].astype(F32) + norm_back(
        second_grad * gains[1], normed_second, inverse_second
    )
    gain_second_part = jnp.sum(second_grad * normed_second, axis=0)
    residual_low = low(residual_grad)

    first_up = send(residual_low, upward)
    first_down = send(residual_low, downward) if places > 2 else first_up
    up_grad = split_rows(mul_tn(after(second_all, residual_low), up_low_all))
    down_grad = down_gradient(after(hidden_all, residual_low), upstream_all, row_parts)
    out_parts = pair_sums(result_own, result_other)
    first_up, first_down, up_grad, down_grad, *out_parts = together(
        first_up, first_down, up_grad, down_grad, *out_parts
    )
    up_sum = scatter(up_grad)
    down_sum = scatter(down_grad)
    residual_slots = [residual_low, first_up]
    while len(residual_slots) < places - 1:
        residual_slots.append(send(residual_slots[-1], upward))
    if places > 2:
        residual_slots.append(first_down)
    residual_others = [swapped(item) for item in (residual_low, first_up, first_down)]
    gate_update = update(state[4], after(gate_sum, first_up))
    released = together(*residual_slots, *residual_others, *gate_update)
    residual_slots, residual_others = released[:places], list(released[places : places + 3])
    gate_update = released[places + 3 :]
    passed = send(out_parts[1], upward)
    residual_others[2:2] = [swapped(item) for item in residual_slots[2 : places - 1]]
    residual_shards = []
    for pair in zip(residual_slots, residual_others):
        residual_shards += pair
    out_grad, output_grad = output_back(output_full, attended, residual_shards, row_parts)
    out_grad, output_grad, passed = together(out_grad, output_grad, passed)
    hops = 2
    if places > 3:
        passed = send(low(out_parts[hops].astype(F32) + passed.astype(F32)), upward)
        hops += 1
    output_items = row_exchange(output_grad)
    qkv_low = attend_back(saved, out_grad, *layout, *sizes)
    qkv_low, passed, *output_items = together(qkv_low, passed, *output_items)

    while hops < places:
        passed = send(low(out_parts[hops].astype(F32) + passed.astype(F32)), upward)
        hops += 1
    parts = spread_parts(qkv_low, qkv_turned, block_parts)
    query_grad, kv_grad, gain_first_part = projection_grad(
        after(qkv_low, parts[0]), scaled_first, qkv_turned, base, row_parts, block_parts
    )
    query_grad, kv_grad, gain_first_part, passed, *parts = together(
        query_grad, kv_grad, gain_first_part, passed, *parts
    )
    own_parts, other_parts = parts[0::2], parts[1::2]
    part, = together(*pair_sums(own_parts[1:2], other_parts[1:2]))
    result = residual + out_parts[0].astype(F32) + passed.astype(F32)
    gain_parts = jnp.stack([gain_first_part[0] / gains[0, 0], gain_second_part])
    gain_parts = gain_parts.reshape(2, row_parts, block_parts, gain_width).transpose(2, 1, 0, 3)
    gain_parts = low(gain_parts).reshape(block_parts, row_parts, 2 * gain_width)
    gain_parts = jnp.pad(
        gain_parts, ((0, 0), (0, spare - row_parts), (0, head_pair - 2 * gain_width))
    )
    kv_grad = jnp.concatenate([kv_grad, gain_parts], axis=1)

    updates = [None] * 7
    updates[4] = gate_update
    for step in range(2, places + 1):
        work = []
        if step == 2:
            work = [
                lax.all_to_all(kv_grad, "blk", 0, 0),
                *pair_sums(own_parts[2:], other_parts[2:]),
                *pair_sums(own_parts[:1], other_parts[:1]),
                low(result)[None],
                *update(state[5], after(up_sum, part)),
            ]
        elif step == 3:
            kv_back = kv_back.astype(F32)
            gain_back = jnp.sum(kv_back[:, key_in : key_in + row_parts, : 2 * gain_width], axis=0)
            kv_back = kv_back[:, :key_in].reshape(KV_HEADS, shares, key_in, head_pair)
            kv_back = jnp.sum(kv_back, axis=1)
            kv_back = kv_back.reshape(row_parts, key_out // HEAD_DIM, key_in, 2, HEAD_DIM)
            kv_back = kv_back.transpose(0, 3, 2, 1, 4).reshape(row_parts, 2 * key_in, key_out)
            gain_back = jnp.pad(
                gain_back[:, None, :], ((0, 0), (0, spare - 1), (0, key_out - 2 * gain_width))
            )
            kv_back = low(jnp.concatenate([kv_back, gain_back], axis=1))
            work = [
                *row_exchange(kv_back),
                *row_exchange(query_grad),
                *update(state[6], after(down_sum, part)),
            ]
        elif step == 4:
            kv_sum = row_sum(kv_items)
            gains_sum = kv_sum[2 * key_in, : 2 * gain_width].reshape(2, gain_width)
            small = [
                row_sum(query_items),
                kv_sum[:key_in],
                kv_sum[key_in : 2 * key_in],
                row_sum(output_items),
            ]
            for number, gradient in enumerate(small):
                work += update(state[number], after(gradient, part))
        released = together(send(part, upward), *work)
        work = released[1:]
        if step == 2:
            kv_back = work[0]
            first_parts = [work[places - 1], None, *work[1 : places - 1]]
            block_out = work[places]
            updates[5] = work[1 + places :]
        elif step == 3:
            kv_items = work[:row_parts]
            query_items = work[row_parts : 2 * row_parts]
            updates[6] = work[2 * row_parts :]
        elif step == 4:
            for number in range(4):
                updates[number] = work[4 * number : 4 * number + 4]
        added = first_parts[step % places].astype(F32) + released[0].astype(F32)
        part = low(added)
    normed_first, inverse_first = norm(resid)
    input_grad = residual_grad + norm_back(added * gains[0], normed_first, inverse_first)
    outs = [block_out, input_grad[None]]
    for item in updates:
        outs.extend(item)
    outs.extend(adam_step(gains_sum, norm_gains, gain_first, gain_second))
    return tuple(outs)


def solution(mesh):
    tokens_placed = P("row", "blk", None)
    gains_placed = P(None, ("row", "blk"))
    blocks_placed = P(("row", "blk"), None, None)
    return jax.shard_map(
        shards,
        mesh=mesh,
        in_specs=(tokens_placed, tokens_placed, P("row", None))
        + (gains_placed,) * 3
        + (blocks_placed,) * 35,
        out_specs=(tokens_placed,) * 2 + (blocks_placed,) * 28 + (gains_placed,) * 3,
        check_vma=False,
    )
```
